128 devices in a mesh: dp: 32 (over y, x, core), tensor: 4 (over z).
Axes of the slice: x: 4, y: 4, z: 4, core: 2. Of those that a mesh axis runs over, the one named last changes fastest.
Arguments:
- out_grad: bfloat16 [65536, 2048], P('dp'), may hold values from -0.046875 to 0.046875
- inputs: bfloat16 [65536, 8192], P('dp', 'tensor'), may hold values from -6 to 6
- weights: float32 [2048, 8192], P('dp', 'tensor'), may hold values from -60 to 60
- moment: float32 [2048, 8192], P('dp', 'tensor'), may hold values from -3 to 3
- second: float32 [2048, 8192], P('dp', 'tensor'), may hold values from 0.05 to 2
Outputs:
- new_weights: float32 [2048, 8192], P('dp', 'tensor')
- new_moment: float32 [2048, 8192], P('dp', 'tensor')
- new_second: float32 [2048, 8192], P('dp', 'tensor')
The draws below stay inside these ranges and needn't reach their ends.
All inputs are finite; a program needn't handle non-finite values.
Results may differ from the reference program's by a relative error of at most 0.0003.
Values sent between devices are 32-bit elements; how exact they have to be, the bound alone decides.
No kernel may reach another device: no remote copies, remote signals or barrier semaphores. Data moves between devices by JAX's collectives and lax.ppermute only.
A program may use at most 128 MiB of HBM per device.

```python
import math
import jax
import jax.numpy as jnp
from jax import lax

D = 8192
ROWS = 2048
TOKENS = 65536


def draw_weights(key, part):
    key = jax.random.fold_in(key, 7)
    first, col_key, row_key = jax.random.split(key, 3)
    ramp = 3.0 ** (jnp.arange(D, dtype=jnp.float32) / D)
    col_scale = 10.0 ** jax.random.uniform(col_key, (1, D), jnp.float32)
    row_scale = 10.0 ** jax.random.uniform(row_key, (ROWS, 1), jnp.float32)
    base = jnp.clip(jax.random.normal(first, (ROWS, D), jnp.float32), -6.0, 6.0)
    return 0.03 * base * ramp[None, :] * col_scale * row_scale


def spiked(array, own_key, source, target, parts, factor):
    owner, partner = [(jnp.arange(array.shape[dim]) // (array.shape[dim] // parts)).reshape([-1 if axis == dim else 1 for axis in range(array.ndim)]) for dim in (source, target)]
    chosen = jax.random.permutation(own_key, parts)[partner]
    strong = (owner == chosen) | (owner == (partner + parts // 2) % parts)
    return jnp.where(strong, factor * array, array)


def block_scale(key, dims, pieces, least, largest):
    level, own = 1.0, jax.random.fold_in(key, 6)
    for position, parts in pieces:
        draws = jnp.exp(jax.random.uniform(jax.random.fold_in(own, position), (parts,), jnp.float32, least / len(pieces), largest / len(pieces)))
        level = level * jnp.repeat(draws, dims[position] // parts).reshape([-1 if axis == position else 1 for axis in range(len(dims))])
    return level


def scatter_about(stream_key, dims, spread, reach, cuts=(), kind=jnp.bfloat16):
    entries = spread * jax.random.normal(stream_key, dims, jnp.float32)
    if cuts:
        entries = entries * block_scale(stream_key, dims, cuts, -0.22, 0.18)
    return jnp.clip(entries, -reach, reach).astype(kind)


def gaussian_with(own_key, shape, deviation, reach, cuts, heavy, kind=jnp.bfloat16):
    values = deviation * jax.random.normal(own_key, shape, jnp.float32)
    if cuts:
        values = values * block_scale(own_key, shape, cuts, -0.22, 0.18)
    return jnp.clip(spiked(values, jax.random.fold_in(own_key, 3), *heavy), -reach, reach).astype(kind)


def setup_inputs(seed: int = 0) -> dict:
    streams_of = jax.random.split(jax.random.key(seed), 6)
    return {
        "out_grad": gaussian_with(streams_of[0], (TOKENS, ROWS), TOKENS ** -0.5, 0.046875, ((0, 32),), (0, 1, 32, 2.75)),
        "inputs": scatter_about(streams_of[1], (TOKENS, D), 1.0, 6.0, ((0, 32), (1, 4))),
        "weights": draw_weights(jax.random.fold_in(streams_of[5], 71), 0),
        "moment": scatter_about(streams_of[3], (ROWS, D), 0.3, 3.0, ((0, 32), (1, 4)), jnp.float32),
        "second": jnp.clip(jnp.exp(math.log(2.0) - 3.6888794 * jax.random.uniform(streams_of[4], (ROWS, D), jnp.float32) ** block_scale(streams_of[4], (ROWS, D), ((0, 32), (1, 4)), -0.2, 0.2)), 0.05, 2.0),
    }


def finish(grad, weights, moment, second):
    new_moment = 0.9 * moment + 0.1 * grad
    new_second = 0.95 * second + 0.05 * grad * grad
    step_size = 0.3 * (new_moment / (1.0 - 0.9 ** 10))
    moved = weights - step_size / (jnp.sqrt(new_second / (1.0 - 0.95 ** 10)) + 1e-08)
    return (moved, new_moment, new_second)

def reference(out_grad, inputs, weights, moment, second):
    grad = lax.dot_general(out_grad, inputs, (((0,), (0,)), ((), ())), preferred_element_type=jnp.float32)
    moved, new_moment, new_second = finish(grad, weights, moment, second)
    mean_square = lax.optimization_barrier(jnp.mean(moved * moved, axis=1, keepdims=True))
    new_weights = moved / jnp.sqrt(mean_square + 1e-06)
    return (new_weights, new_moment, new_second)
```

```python
import functools

import jax
import jax.numpy as jnp
from jax import lax
from jax.experimental import pallas as pl
from jax.experimental.pallas import tpu as pltpu
from jax.sharding import PartitionSpec as P

F32 = jnp.float32
BF16 = jnp.bfloat16
MIB = 2**20
VMEM = pltpu.VMEM
ROWS = 64
TILES = 16
CHAINS = ((0, 1024, (0, 1, 2, 3)), (1024, 1024, (1, 0, 3, 2)))

RING_A = (1, 0, 3, 2)
RING_B = (3, 2, 1, 0)


def device_index(y, x, core):
    return (y * 4 + x) * 2 + core


def swap_pairs(kind):
    partner = RING_B if kind % 2 else RING_A
    pairs = []
    for y in range(4):
        for x in range(4):
            for core in range(2):
                along_x = (core == 0) == (kind < 2)
                to = (y, partner[x]) if along_x else (partner[y], x)
                pairs.append((device_index(y, x, core), device_index(*to, core)))
    return pairs


SWAPS = [swap_pairs(kind) for kind in range(4)]
CORE_SWAP = [(i, i ^ 1) for i in range(32)]
Z_SWAPS = (list(enumerate(RING_A)), list(enumerate(RING_B)))


def params(mib, **more):
    return pltpu.CompilerParams(vmem_limit_bytes=mib * MIB, **more)


def in_vmem():
    return pl.BlockSpec(memory_space=VMEM)


def gray(i):
    high = lax.shift_right_logical(i, 1)
    return high ^ (i & 1), high


def prep_kernel(tiles, out_grad, turned):
    me = lax.axis_index("dp")
    core = me & 1
    my_x = gray(lax.shift_right_logical(me, 1) & 3)
    my_y = gray(lax.shift_right_logical(me, 3))
    for k in range(tiles):
        tile = pl.program_id(0) * tiles + k
        xa, xb = [a ^ b for a, b in zip(gray(tile & 3), my_x)]
        ya, yb = [a ^ b for a, b in zip(gray(lax.shift_right_logical(tile, 2)), my_y)]
        place0 = xa * 8 + xb * 4 + ya * 2 + yb + 16 * (1 - core)
        place1 = ya * 8 + yb * 4 + xa * 2 + xb + 16 * core
        block = out_grad[:, k * 128 : (k + 1) * 128].T
        turned[pl.ds(place0, 1)] = block[:ROWS][None]
        turned[pl.ds(place1, 1)] = block[ROWS:][None]


def prep(out_grad):
    tokens, rows = out_grad.shape
    tiles = 2
    return pl.pallas_call(
        functools.partial(prep_kernel, tiles),
        grid=(TILES // tiles,),
        out_shape=pltpu.VMEM((2 * TILES, ROWS, tokens), BF16),
        in_specs=[pl.BlockSpec((tokens, tiles * 128), lambda i: (0, i))],
        out_specs=in_vmem(),
        compiler_params=params(16),
        name="prep",
    )(out_grad)


def gemm_kernel(blocks, first, width, add, *refs):
    if add:
        turned, inputs, received, out = refs
    else:
        turned, inputs, out = refs
    row = 0
    for lo, hi in blocks:
        left = turned[lo:hi].reshape((hi - lo) * ROWS, turned.shape[2])
        for col in range(0, width, 256):
            part = jnp.dot(
                left, inputs[:, first + col : first + col + 256], preferred_element_type=F32
            )
            if add:
                part = part + received[row : row + (hi - lo) * ROWS, col : col + 256]
            out[row : row + (hi - lo) * ROWS, col : col + 256] = part
        row += (hi - lo) * ROWS


def gemm(name, turned, inputs, blocks, first, width, received=None):
    rows = sum(hi - lo for lo, hi in blocks) * ROWS
    tokens = inputs.shape[0]
    args = (turned, inputs) + (() if received is None else (received,))
    return pl.pallas_call(
        functools.partial(gemm_kernel, blocks, first, width, received is not None),
        out_shape=pltpu.VMEM((rows, width), F32),
        in_specs=[in_vmem()] * len(args),
        out_specs=in_vmem(),
        compiler_params=params(4),
        cost_estimate=pl.CostEstimate(
            flops=2 * rows * width * tokens, bytes_accessed=rows * width * 4, transcendentals=0
        ),
        name=name,
    )(*args)


def blocks_of(order, side, sent):
    base = 0 if side == "sib" else TILES
    if order[0] == 0:
        lo = base + 8 * sent
        return ((lo, lo + 8),)
    lo = base + 4 * sent
    return ((lo, lo + 4), (lo + 8, lo + 12))


def finish_kernel(kept, came, weights, moment, second, moved, new_moment, new_second, sums):
    total = jnp.zeros((ROWS, 128), F32)
    for (first, width, _), a, b in zip(CHAINS, kept, came):
        for col in range(0, width, 128):
            here = (slice(None), slice(first + col, first + col + 128))
            grad = a[:, col : col + 128] + b[:, col : col + 128]
            m = 0.9 * moment[here] + 0.1 * grad
            v = 0.95 * second[here] + 0.05 * grad * grad
            step = 0.3 * (m / (1.0 - 0.9**10))
            w = weights[here] - step / (jnp.sqrt(v / (1.0 - 0.95**10)) + 1e-08)
            new_moment[here] = m
            new_second[here] = v
            moved[here] = w
            total = total + w * w
    sums[...] = jnp.broadcast_to(jnp.sum(total, axis=1, keepdims=True), sums.shape)


def finish(kept, came, weights, moment, second):
    n = len(CHAINS)

    def kernel(*refs):
        finish_kernel(refs[:n], refs[n : 2 * n], *refs[2 * n :])

    shape = jax.ShapeDtypeStruct(weights.shape, F32)
    return pl.pallas_call(
        kernel,
        out_shape=(pltpu.VMEM(weights.shape, F32), shape, shape, pltpu.VMEM((ROWS, 128), F32)),
        in_specs=[in_vmem()] * (2 * n + 3),
        out_specs=[in_vmem()] * 4,
        compiler_params=params(8),
        name="finish",
    )(*kept, *came, weights, moment, second)


def rescale_kernel(width, moved, mine, theirs, out):
    scale = lax.rsqrt((mine[...] + theirs[...]) / width + 1e-06)
    for col in range(0, moved.shape[1], 128):
        out[:, col : col + 128] = moved[:, col : col + 128] * scale


def rescale(moved, mine, theirs, width):
    return pl.pallas_call(
        functools.partial(rescale_kernel, width),
        out_shape=jax.ShapeDtypeStruct(moved.shape, F32),
        in_specs=[in_vmem()] * 3,
        out_specs=in_vmem(),
        compiler_params=params(4),
        name="rescale",
    )(moved, mine, theirs)


def on_device(out_grad, inputs, weights, moment, second):
    width = weights.shape[1] * lax.axis_size("tensor")
    inputs = pltpu.with_memory_space_constraint(inputs, VMEM)
    turned = prep(out_grad)
    sent = []
    for i, (first, cols, order) in enumerate(CHAINS):
        part = gemm(f"sib_sent_{i}", turned, inputs, blocks_of(order, "sib", 1), first, cols)
        sent.append(lax.ppermute(part, "dp", CORE_SWAP))
    came = []
    for i, (first, cols, order) in enumerate(CHAINS):
        part = gemm(f"own_sent_{i}", turned, inputs, blocks_of(order, "own", 1), first, cols, sent[i])
        came.append(lax.ppermute(part, "dp", SWAPS[order[0]]))
    other = []
    for i, (first, cols, order) in enumerate(CHAINS):
        part = gemm(f"sib_kept_{i}", turned, inputs, blocks_of(order, "sib", 0), first, cols)
        other.append(lax.ppermute(part, "dp", CORE_SWAP))
    kept = []
    for i, (first, cols, order) in enumerate(CHAINS):
        kept.append(gemm(f"own_kept_{i}", turned, inputs, blocks_of(order, "own", 0), first, cols, other[i]))
    for step in range(1, 4):
        for i, (first, cols, order) in enumerate(CHAINS):
            size = kept[i].shape[0] // 2
            a, b = kept[i], came[i]
            if step == 2 and order[2] == 3:
                a, b = [z.reshape(2, 2, ROWS, cols) for z in (a, b)]
                up, down = [(a[:, k] + b[:, k]).reshape(size, cols) for k in (1, 0)]
            else:
                up, down = a[size:] + b[size:], a[:size] + b[:size]
            came[i] = lax.ppermute(up, "dp", SWAPS[order[step]])
            kept[i] = down
    moved, new_moment, new_second, sums = finish(kept, came, weights, moment, second)
    sums = sums + lax.ppermute(sums, "tensor", Z_SWAPS[0])
    theirs = lax.ppermute(sums, "tensor", Z_SWAPS[1])
    return rescale(moved, sums, theirs, width), new_moment, new_second


def solution(mesh):
    spec = P("dp", "tensor")
    return jax.shard_map(
        on_device,
        mesh=mesh,
        in_specs=(P("dp", None), spec, spec, spec, spec),
        out_specs=(spec, spec, spec),
        check_vma=False,
    )
```

```python
import functools

import jax
import jax.numpy as jnp
from jax import lax
from jax.experimental import pallas as pl
from jax.experimental.pallas import tpu as pltpu
from jax.sharding import PartitionSpec as P

F32 = jnp.float32
BF16 = jnp.bfloat16
MIB = 2**20
VMEM = pltpu.VMEM
ROWS = 64
TILES = 16
STRIPS = 8
FORTH, BACK = (0, 1, 2, 3), (1, 0, 3, 2)
CHAINS = ((0, 0, 768, FORTH), (1, 0, 768, BACK), (0, 768, 256, FORTH), (1, 768, 256, BACK))
ORDER = (
    "s1:0", "s1:1", "o1:0", "o1:1", "s0:01", "s1:23", "op:0", "op:1",
    "o1:2", "o1:3", "s0:23", "x2:0", "x2:1", "c2:0", "c2:1", "o0:2",
    "o0:3", "c2:2", "c2:3", "c3:02", "c3:13", "c4:0", "c4:1", "f:0",
    "f:1",
)
COSTS = {"x2:1": 20000000000, "c2:1": 10000000000, "f:0": 1000000000}

RING_A = (1, 0, 3, 2)
RING_B = (3, 2, 1, 0)


def device_index(y, x, core):
    return (y * 4 + x) * 2 + core


def swap_pairs(kind):
    partner = RING_B if kind % 2 else RING_A
    pairs = []
    for y in range(4):
        for x in range(4):
            for core in range(2):
                along_x = (core == 0) == (kind < 2)
                to = (y, partner[x]) if along_x else (partner[y], x)
                pairs.append((device_index(y, x, core), device_index(*to, core)))
    return pairs


SWAPS = [swap_pairs(kind) for kind in range(4)]
CORE_SWAP = [(i, i ^ 1) for i in range(32)]
Z_SWAPS = [list(enumerate(ring)) for ring in (RING_A, RING_B, (2, 3, 0, 1))]


def params(mib, **more):
    return pltpu.CompilerParams(vmem_limit_bytes=mib * MIB, **more)


def in_vmem():
    return pl.BlockSpec(memory_space=VMEM)


def gray(i):
    high = i >> 1
    return high ^ (i & 1), high


def half_copies(inputs, half, which, arrived, first):
    rows, width = half.shape[0] // STRIPS, half.shape[1]
    return [
        pltpu.make_async_copy(
            inputs.at[k * rows : (k + 1) * rows, which * width : (which + 1) * width],
            half.at[k * rows : (k + 1) * rows],
            arrived.at[first + k],
        )
        for k in range(STRIPS)
    ]


def prep_kernel(pieces, out_grad, inputs, turned, left, right, product, held, arrived):
    strips = held.shape[0]
    tiles = TILES // strips
    width = tiles * 128
    copies = [
        pltpu.make_async_copy(
            out_grad.at[:, k * width : (k + 1) * width], held.at[k], arrived.at[k]
        )
        for k in range(strips)
    ]
    copies += half_copies(inputs, left, 0, arrived, strips)
    copies += half_copies(inputs, right, 1, arrived, strips + STRIPS)
    for copy in copies:
        copy.start()
    me = lax.axis_index("dp")
    core = me & 1
    my_x = gray((me >> 1) & 3)
    my_y = gray(me >> 3)
    for tile in range(TILES):
        if tile % tiles == 0:
            copies[tile // tiles].wait()
        xa, xb = [a ^ b for a, b in zip(gray(tile & 3), my_x)]
        ya, yb = [a ^ b for a, b in zip(gray(tile >> 2), my_y)]
        place0 = xa * 8 + xb * 4 + ya * 2 + yb + 16 * (1 - core)
        place1 = ya * 8 + yb * 4 + xa * 2 + xb + 16 * core
        col = tile % tiles * 128
        block = held[tile // tiles, :, col : col + 128].T
        turned[pl.ds(place0, 1)] = block[:ROWS][None]
        turned[pl.ds(place1, 1)] = block[ROWS:][None]
    for copy in copies[strips : strips + STRIPS]:
        copy.wait()
    gemm_kernel(pieces, 0, 0, turned, left, right, product)
    for copy in copies[strips + STRIPS :]:
        copy.wait()


def prep(out_grad, inputs, pieces):
    tokens, rows = out_grad.shape
    strips = 8
    half = VMEM((tokens, inputs.shape[1] // 2), BF16)
    product = sum(hi - lo for (lo, hi), *_ in pieces) * ROWS, pieces[0][3]
    return pl.pallas_call(
        functools.partial(prep_kernel, pieces),
        out_shape=(VMEM((2 * TILES, ROWS, tokens), BF16), half, half, VMEM(product, F32)),
        in_specs=[pl.BlockSpec(memory_space=pl.ANY)] * 2,
        out_specs=[in_vmem()] * 4,
        scratch_shapes=[
            VMEM((strips, tokens, rows // strips), BF16),
            pltpu.SemaphoreType.DMA((strips + 2 * STRIPS,)),
        ],
        compiler_params=params(12),
        name="prep",
    )(out_grad, inputs)


def call(kernel, args, after, flops, **more):
    extra = () if after is None else (after,)

    def run(*refs):
        kernel(*refs[: len(args)], *refs[len(args) + len(extra) :])

    specs = [in_vmem()] * len(args) + [pl.BlockSpec(memory_space=pl.ANY)] * len(extra)
    cost = pl.CostEstimate(flops=flops, bytes_accessed=1, transcendentals=0)
    return pl.pallas_call(run, in_specs=specs, cost_estimate=cost, **more)(*args, *extra)


def gemm_kernel(pieces, offset, count, turned, *refs):
    halves, received, outs = refs[:2], refs[2 : 2 + count], refs[2 + count :]
    row = 0
    for (lo, hi), half, first, width in pieces:
        rows = (hi - lo) * ROWS
        left = turned[lo:hi].reshape(rows, turned.shape[2])
        out, at = outs[row // outs[0].shape[0]], row % outs[0].shape[0]
        for col in range(0, width, 256):
            right = halves[half][:, first + col : first + col + 256]
            part = jnp.dot(left, right, preferred_element_type=F32)
            if received:
                from_row = offset + row
                ref, come = received[from_row // received[0].shape[0]], from_row % received[0].shape[0]
                part = part + ref[come : come + rows, col : col + 256]
            out[at : at + rows, col : col + 256] = part
        row += rows


def gemm(name, after, cost, turned, halves, pieces, shares=1, received=(), offset=0):
    rows = sum(hi - lo for (lo, hi), *_ in pieces) * ROWS
    return call(
        functools.partial(gemm_kernel, pieces, offset, len(received)),
        (turned, *halves, *received),
        after,
        cost,
        out_shape=[VMEM((rows // shares, pieces[0][3]), F32)] * shares,
        out_specs=[in_vmem()] * shares,
        compiler_params=params(4),
        name=name,
    )


def pieces_of(chain, side, sent):
    *columns, order = CHAINS[chain]
    base = 0 if side == "s" else TILES
    if order[0] == 0:
        spans = ((base + 8 * sent, base + 8 * sent + 8),)
    else:
        spans = tuple((lo, lo + 4) for lo in (base + 4 * sent, base + 4 * sent + 8))
    return [(span, *columns) for span in spans]


def quarters(pieces):
    return [((at, at + 4), *columns) for (lo, hi), *columns in pieces for at in range(lo, hi, 4)]


def add_kernel(a, b, out):
    out[...] = a[...] + b[...]


def add(name, after, cost, a, b):
    return call(
        add_kernel,
        (a, b),
        after,
        cost,
        out_shape=VMEM(a.shape, F32),
        out_specs=in_vmem(),
        compiler_params=params(4),
        name=name,
    )


def combine_kernel(split, offset, *refs):
    *pairs, up, down = refs
    col = 0
    for kept, came in zip(pairs[::2], pairs[1::2]):
        rows, width = kept.shape
        size = rows // (2 * split)
        for i in range(split):
            for half, out in ((0, down), (1, up)):
                lo = (2 * i + half) * size
                out[i * size : (i + 1) * size, col : col + width] = (
                    kept[lo : lo + size] + came[offset + lo : offset + lo + size]
                )
        col += width


def combine(name, after, cost, split, pairs, offset=0):
    half = VMEM((pairs[0][0].shape[0] // 2, sum(kept.shape[1] for kept, _ in pairs)), F32)
    return call(
        functools.partial(combine_kernel, split, offset),
        [array for pair in pairs for array in pair],
        after,
        cost,
        out_shape=(half, half),
        out_specs=[in_vmem()] * 2,
        compiler_params=params(4),
        name=name,
    )


def finish_kernel(first, kept, came, weights, moment, second, *outs):
    moved, new_moment, new_second, sums = outs
    total = jnp.zeros((ROWS, 128), F32)
    for col in range(0, kept.shape[1], 128):
        there = (slice(None), slice(col, col + 128))
        here = (slice(None), slice(first + col, first + col + 128))
        grad = kept[there] + came[there]
        m = 0.9 * moment[here] + 0.1 * grad
        v = 0.95 * second[here] + 0.05 * grad * grad
        step = 0.3 * (m / (1.0 - 0.9**10))
        w = weights[here] - step / (jnp.sqrt(v / (1.0 - 0.95**10)) + 1e-08)
        new_moment[there] = m
        new_second[there] = v
        moved[there] = w
        total = total + w * w
    sums[...] = jnp.broadcast_to(jnp.sum(total, axis=1, keepdims=True), sums.shape)


def finish(name, after, cost, first, kept, came, weights, moment, second):
    shape = VMEM(kept.shape, F32)
    return call(
        functools.partial(finish_kernel, first),
        (kept, came, weights, moment, second),
        after,
        cost,
        out_shape=(shape, shape, shape, VMEM((ROWS, 128), F32)),
        out_specs=[in_vmem()] * 4,
        compiler_params=params(4),
        name=name,
    )


def join_kernel(a, b, c, d, ab, cd):
    width = a.shape[1]
    for left, right, out in ((a, b, ab), (c, d, cd)):
        out[:, :width] = left[...]
        out[:, width:] = right[...]


def join(after, moments, seconds):
    rows, width = moments[0].shape
    return call(
        join_kernel,
        (*moments, *seconds),
        after,
        1,
        out_shape=[jax.ShapeDtypeStruct((rows, 2 * width), F32)] * 2,
        out_specs=[in_vmem()] * 2,
        compiler_params=params(4),
        name="join",
    )


def rescale_kernel(width, a, b, *refs):
    *sums, out = refs
    total = sums[0][...]
    for other in sums[1:]:
        total = total + other[...]
    scale = lax.rsqrt(total / width + 1e-06)
    for k, moved in enumerate((a, b)):
        for col in range(0, moved.shape[1], 128):
            at = k * moved.shape[1] + col
            out[:, at : at + 128] = moved[:, col : col + 128] * scale


def rescale(moved, sums, width):
    rows, half = moved[0].shape
    return pl.pallas_call(
        functools.partial(rescale_kernel, width),
        out_shape=jax.ShapeDtypeStruct((rows, 2 * half), F32),
        in_specs=[in_vmem()] * (2 + len(sums)),
        out_specs=in_vmem(),
        compiler_params=params(4),
        name="rescale",
    )(*moved, *sums)


def on_device(out_grad, inputs, weights, moment, second):
    width = weights.shape[1] * lax.axis_size("tensor")
    out_grad, inputs = [pltpu.with_memory_space_constraint(z, pltpu.HBM) for z in (out_grad, inputs)]
    first = pieces_of(int(ORDER[0][-1]), "s", 1)
    turned, *halves, product = prep(out_grad, inputs, first)
    n = len(CHAINS)
    received, kept, came = {}, [None] * n, [None] * n
    late, done = {}, {}
    last = None
    for item in ORDER:
        what, which = item.split(":")
        which, _, shares = which.partition("/")
        shares = int(shares or 1)
        name = f"{what}_{which}"
        cost = COSTS.get(what + ":" + which, 1)
        chains = [int(i) for i in which]
        i = chains[0]
        order = CHAINS[i][3]
        if what[0] in "so":
            sent = int(what[1] == "1")
            pieces = [piece for j in chains for piece in pieces_of(j, what[0], sent)]
            if what[0] == "s":
                if shares > 1:
                    pieces = quarters(pieces)
                if last is None:
                    parts = [product]
                else:
                    parts = gemm(name, last, cost, turned, halves, pieces, shares)
                last = parts[0]
                over = [lax.ppermute(part, "dp", CORE_SWAP) for part in parts]
                for k, j in enumerate(chains):
                    received[j, sent] = over, k * (TILES // 2) * ROWS
            elif what[1] == "p":
                [last] = gemm(name, last, cost, turned, halves, pieces)
                kept[i] = last
            else:
                over, offset = received[i, sent]
                if len(over) > 1:
                    pieces = quarters(pieces)
                [last] = gemm(name, last, cost, turned, halves, pieces, 1, over, offset)
                if sent:
                    came[i] = lax.ppermute(last, "dp", SWAPS[order[0]])
                else:
                    kept[i] = last
        elif what == "x2":
            last = kept[i] = add(name, last, cost, kept[i], came[i])
            [came[i]], late[i] = received[i, 0]
        elif what == "f":
            first = i * kept[i].shape[1]
            done[i] = finish(name, last, cost, first, kept[i], came[i], weights, moment, second)
            last = done[i][3]
        else:
            step = int(what[1])
            split = 2 if step == 3 and order[2] == 3 else 1
            pairs = [(kept[j], came[j]) for j in chains]
            last, kept[i] = combine(name, last, cost, split, pairs, late.pop(i, 0))
            came[i] = lax.ppermute(last, "dp", SWAPS[order[step - 1]])
    moved, moments, seconds, sums = zip(done[0], done[1])
    sums = sums[0] + sums[1]
    new_moment, new_second = join(sums, moments, seconds)
    sums = [sums] + [lax.ppermute(sums, "tensor", swap) for swap in Z_SWAPS]
    return rescale(moved, sums, width), new_moment, new_second


def solution(mesh):
    spec = P("dp", "tensor")
    return jax.shard_map(
        on_device,
        mesh=mesh,
        in_specs=(P("dp", None), spec, spec, spec, spec),
        out_specs=(spec, spec, spec),
        check_vma=False,
    )
```

```python
import functools

import jax
import jax.numpy as jnp
from jax import lax
from jax.experimental import pallas as pl
from jax.experimental.pallas import tpu as pltpu
from jax.sharding import PartitionSpec as P

F32 = jnp.float32
BF16 = jnp.bfloat16
MIB = 2**20
VMEM = pltpu.VMEM
ROWS = 64
TILES = 16
STRIPS = 8
FORTH, BACK = (0, 1, 2, 3), (1, 0, 3, 2)
CHAINS = ((0, 0, 768, FORTH), (1, 0, 768, BACK), (0, 768, 256, FORTH), (1, 768, 256, BACK))
PARTS = [sum(chain[2] for chain in CHAINS if chain[0] == part) for part in (0, 1)]
ORDER = (
    "s1:0", "s1:1", "oq:0", "a1:0", "o1:1", "s0:01", "s1:23", "op:0",
    "op:1", "o1:2", "o1:3", "s0:23", "x2:0", "x2:1", "c2:1", "c2:0",
    "o0:2", "o0:3", "c2:3", "c2:2", "c3:13", "c3:02", "c4:1", "c4:0",
    "f:1", "f:0",
)
COSTS = {"x2:1": 20000000000, "c2:0": 10000000000, "f:1": 1000000000}

RING_A = (1, 0, 3, 2)
RING_B = (3, 2, 1, 0)


def device_index(y, x, core):
    return (y * 4 + x) * 2 + core


def swap_pairs(kind):
    partner = RING_B if kind % 2 else RING_A
    pairs = []
    for y in range(4):
        for x in range(4):
            for core in range(2):
                along_x = (core == 0) == (kind < 2)
                to = (y, partner[x]) if along_x else (partner[y], x)
                pairs.append((device_index(y, x, core), device_index(*to, core)))
    return pairs


SWAPS = [swap_pairs(kind) for kind in range(4)]
CORE_SWAP = [(i, i ^ 1) for i in range(32)]
Z_SWAPS = [list(enumerate(ring)) for ring in (RING_A, RING_B, (2, 3, 0, 1))]


def params(mib, **more):
    return pltpu.CompilerParams(vmem_limit_bytes=mib * MIB, **more)


def in_vmem():
    return pl.BlockSpec(memory_space=VMEM)


def gray(i):
    high = i >> 1
    return high ^ (i & 1), high


def half_copies(inputs, half, which, arrived, first):
    rows, width = half.shape[0] // STRIPS, half.shape[1]
    first_col = which * (inputs.shape[1] - width)
    return [
        pltpu.make_async_copy(
            inputs.at[k * rows : (k + 1) * rows, first_col : first_col + width],
            half.at[k * rows : (k + 1) * rows],
            arrived.at[first + k],
        )
        for k in range(STRIPS)
    ]


def prep_kernel(pieces, out_grad, inputs, turned, left, right, product, held, arrived):
    strips = held.shape[0]
    tiles = TILES // strips
    width = tiles * 128
    copies = [
        pltpu.make_async_copy(
            out_grad.at[:, k * width : (k + 1) * width], held.at[k], arrived.at[k]
        )
        for k in range(strips)
    ]
    copies += half_copies(inputs, left, 0, arrived, strips)
    copies += half_copies(inputs, right, 1, arrived, strips + STRIPS)
    for copy in copies:
        copy.start()
    me = lax.axis_index("dp")
    core = me & 1
    my_x = gray((me >> 1) & 3)
    my_y = gray(me >> 3)
    for tile in range(TILES):
        if tile % tiles == 0:
            copies[tile // tiles].wait()
        xa, xb = [a ^ b for a, b in zip(gray(tile & 3), my_x)]
        ya, yb = [a ^ b for a, b in zip(gray(tile >> 2), my_y)]
        place0 = xa * 8 + xb * 4 + ya * 2 + yb + 16 * (1 - core)
        place1 = ya * 8 + yb * 4 + xa * 2 + xb + 16 * core
        col = tile % tiles * 128
        block = held[tile // tiles, :, col : col + 128].T
        turned[pl.ds(place0, 1)] = block[:ROWS][None]
        turned[pl.ds(place1, 1)] = block[ROWS:][None]
    for copy in copies[strips : strips + STRIPS]:
        copy.wait()
    gemm_kernel(pieces, 0, 0, turned, left, right, product)
    for copy in copies[strips + STRIPS :]:
        copy.wait()


def prep(out_grad, inputs, pieces):
    tokens, rows = out_grad.shape
    strips = 8
    parts = [VMEM((tokens, cols), BF16) for cols in PARTS]
    product = sum(hi - lo for (lo, hi), *_ in pieces) * ROWS, pieces[0][3]
    return pl.pallas_call(
        functools.partial(prep_kernel, pieces),
        out_shape=(VMEM((2 * TILES, ROWS, tokens), BF16), *parts, VMEM(product, F32)),
        in_specs=[pl.BlockSpec(memory_space=pl.ANY)] * 2,
        out_specs=[in_vmem()] * 4,
        scratch_shapes=[
            VMEM((strips, tokens, rows // strips), BF16),
            pltpu.SemaphoreType.DMA((strips + 2 * STRIPS,)),
        ],
        compiler_params=params(12),
        name="prep",
    )(out_grad, inputs)


def call(kernel, args, after, flops, **more):
    extra = () if after is None else (after,)

    def run(*refs):
        kernel(*refs[: len(args)], *refs[len(args) + len(extra) :])

    specs = [in_vmem()] * len(args) + [pl.BlockSpec(memory_space=pl.ANY)] * len(extra)
    cost = pl.CostEstimate(flops=flops, bytes_accessed=1, transcendentals=0)
    return pl.pallas_call(run, in_specs=specs, cost_estimate=cost, **more)(*args, *extra)


def gemm_kernel(pieces, offset, count, turned, *refs):
    halves, received, outs = refs[:2], refs[2 : 2 + count], refs[2 + count :]
    row = 0
    for (lo, hi), half, first, width in pieces:
        rows = (hi - lo) * ROWS
        left = turned[lo:hi].reshape(rows, turned.shape[2])
        out, at = outs[row // outs[0].shape[0]], row % outs[0].shape[0]
        for col in range(0, width, 256):
            end = min(col + 256, width)
            right = halves[half][:, first + col : first + end]
            part = jnp.dot(left, right, preferred_element_type=F32)
            if received:
                from_row = offset + row
                ref, come = received[from_row // received[0].shape[0]], from_row % received[0].shape[0]
                part = part + ref[come : come + rows, col:end]
            out[at : at + rows, col:end] = part
        if width < out.shape[1]:
            out[at : at + rows, width:] = jnp.zeros((rows, out.shape[1] - width), F32)
        row += rows


def gemm(name, after, cost, turned, halves, pieces, shares=1, received=(), offset=0):
    rows = sum(hi - lo for (lo, hi), *_ in pieces) * ROWS
    return call(
        functools.partial(gemm_kernel, pieces, offset, len(received)),
        (turned, *halves, *received),
        after,
        cost,
        out_shape=[VMEM((rows // shares, max(piece[3] for piece in pieces)), F32)] * shares,
        out_specs=[in_vmem()] * shares,
        compiler_params=params(4),
        name=name,
    )


def pieces_of(chain, side, sent):
    *columns, order = CHAINS[chain]
    base = 0 if side == "s" else TILES
    if order[0] == 0:
        spans = ((base + 8 * sent, base + 8 * sent + 8),)
    else:
        spans = tuple((lo, lo + 4) for lo in (base + 4 * sent, base + 4 * sent + 8))
    return [(span, *columns) for span in spans]


def quarters(pieces):
    return [((at, at + 4), *columns) for (lo, hi), *columns in pieces for at in range(lo, hi, 4)]


def add_kernel(a, b, out):
    out[...] = a[...] + b[...]


def add(name, after, cost, a, b):
    return call(
        add_kernel,
        (a, b),
        after,
        cost,
        out_shape=VMEM(a.shape, F32),
        out_specs=in_vmem(),
        compiler_params=params(4),
        name=name,
    )


def combine_kernel(split, offset, added, *refs):
    *refs, up, down = refs
    col = 0
    for is_sum in added:
        kept = refs.pop(0)
        came = None if is_sum else refs.pop(0)
        rows, width = kept.shape
        size = rows // (2 * split)
        for i in range(split):
            for half, out in ((0, down), (1, up)):
                lo = (2 * i + half) * size
                total = kept[lo : lo + size]
                if came is not None:
                    total = total + came[offset + lo : offset + lo + size, :width]
                out[i * size : (i + 1) * size, col : col + width] = total
        col += width


def combine(name, after, cost, split, pairs, offset=0):
    half = VMEM((pairs[0][0].shape[0] // 2, sum(kept.shape[1] for kept, _ in pairs)), F32)
    added = [came is None for _, came in pairs]
    return call(
        functools.partial(combine_kernel, split, offset, added),
        [array for pair in pairs for array in pair if array is not None],
        after,
        cost,
        out_shape=(half, half),
        out_specs=[in_vmem()] * 2,
        compiler_params=params(4),
        name=name,
    )


def finish_kernel(first, kept, came, weights, moment, second, *outs):
    moved, new_moment, new_second, sums = outs
    total = jnp.zeros((ROWS, 128), F32)
    for col in range(0, kept.shape[1], 128):
        there = (slice(None), slice(col, col + 128))
        here = (slice(None), slice(first + col, first + col + 128))
        grad = kept[there] + came[there]
        m = 0.9 * moment[here] + 0.1 * grad
        v = 0.95 * second[here] + 0.05 * grad * grad
        step = 0.3 * (m / (1.0 - 0.9**10))
        w = weights[here] - step / (jnp.sqrt(v / (1.0 - 0.95**10)) + 1e-08)
        new_moment[there] = m
        new_second[there] = v
        moved[there] = w
        total = total + w * w
    total = jnp.broadcast_to(jnp.sum(total, axis=1, keepdims=True), total.shape)
    sums[...] = total.T[: sums.shape[0]]


def finish(name, after, cost, first, kept, came, weights, moment, second):
    shape = VMEM(kept.shape, F32)
    return call(
        functools.partial(finish_kernel, first),
        (kept, came, weights, moment, second),
        after,
        cost,
        out_shape=(shape, shape, shape, VMEM((8, ROWS), F32)),
        out_specs=[in_vmem()] * 4,
        compiler_params=params(4),
        name=name,
    )


def join_kernel(a, b, c, d, ab, cd):
    width = a.shape[1]
    for left, right, out in ((a, b, ab), (c, d, cd)):
        out[:, :width] = left[...]
        out[:, width:] = right[...]


def join(after, moments, seconds):
    shape = jax.ShapeDtypeStruct((ROWS, sum(PARTS)), F32)
    return call(
        join_kernel,
        (*moments, *seconds),
        after,
        1,
        out_shape=[shape] * 2,
        out_specs=[in_vmem()] * 2,
        compiler_params=params(4),
        name="join",
    )


def rescale_kernel(width, a, b, *refs):
    *sums, out = refs
    total = sums[0][...]
    for other in sums[1:]:
        total = total + other[...]
    scale = lax.rsqrt(total[:1] / width + 1e-06)
    scale = jnp.broadcast_to(scale, (128, ROWS)).T
    at = 0
    for moved in (a, b):
        for col in range(0, moved.shape[1], 128):
            out[:, at + col : at + col + 128] = moved[:, col : col + 128] * scale
        at += moved.shape[1]


def rescale(moved, sums, width):
    return pl.pallas_call(
        functools.partial(rescale_kernel, width),
        out_shape=jax.ShapeDtypeStruct((ROWS, sum(PARTS)), F32),
        in_specs=[in_vmem()] * (2 + len(sums)),
        out_specs=in_vmem(),
        compiler_params=params(4),
        name="rescale",
    )(*moved, *sums)


def on_device(out_grad, inputs, weights, moment, second):
    width = weights.shape[1] * lax.axis_size("tensor")
    out_grad, inputs = [pltpu.with_memory_space_constraint(z, pltpu.HBM) for z in (out_grad, inputs)]
    first = pieces_of(int(ORDER[0][-1]), "s", 1)
    turned, *halves, product = prep(out_grad, inputs, first)
    n = len(CHAINS)
    received, kept, came = {}, [None] * n, [None] * n
    late, own, done = {}, {}, {}
    last = None
    for item in ORDER:
        what, which = item.split(":")
        which, _, shares = which.partition("/")
        shares = int(shares or 1)
        name = f"{what}_{which}"
        cost = COSTS.get(what + ":" + which, 1)
        chains = [int(i) for i in which]
        i = chains[0]
        order = CHAINS[i][3]
        if what[0] in "so":
            sent = int(what[1] == "1")
            pieces = [piece for j in chains for piece in pieces_of(j, what[0], sent)]
            if what[0] == "s":
                if shares > 1:
                    pieces = quarters(pieces)
                if last is None:
                    parts = [product]
                else:
                    parts = gemm(name, last, cost, turned, halves, pieces, shares)
                last = parts[0]
                over = [lax.ppermute(part, "dp", CORE_SWAP) for part in parts]
                for k, j in enumerate(chains):
                    received[j, sent] = over, k * (TILES // 2) * ROWS
            elif what[1] == "p":
                [last] = gemm(name, last, cost, turned, halves, pieces)
                kept[i] = last
            elif what[1] == "q":
                pieces = pieces_of(i, "o", 1)
                [last] = gemm(name, last, cost, turned, halves, pieces)
                own[i] = last
            else:
                over, offset = received[i, sent]
                if len(over) > 1:
                    pieces = quarters(pieces)
                [last] = gemm(name, last, cost, turned, halves, pieces, 1, over, offset)
                if sent:
                    came[i] = lax.ppermute(last, "dp", SWAPS[order[0]])
                else:
                    kept[i] = last
        elif what == "a1":
            last = add(name, last, cost, own[i], *received[i, 1][0])
            came[i] = lax.ppermute(last, "dp", SWAPS[order[0]])
        elif what[0] == "x":
            last = kept[i] = add(name, last, cost, kept[i], came[i])
            came[i] = None
            if what == "x2":
                [came[i]], late[i] = received[i, 0]
        elif what == "f":
            first = i * PARTS[0]
            done[i] = finish(name, last, cost, first, kept[i], came[i], weights, moment, second)
            last = done[i][3]
        else:
            step = int(what[1])
            split = 2 if step == 3 and order[2] == 3 else 1
            pairs = [(kept[j], came[j]) for j in chains]
            last, kept[i] = combine(name, last, cost, split, pairs, late.pop(i, 0))
            came[i] = lax.ppermute(last, "dp", SWAPS[order[step - 1]])
    moved, moments, seconds, sums = zip(done[0], done[1])
    sums = sums[0] + sums[1]
    new_moment, new_second = join(sums, moments, seconds)
    sums = [sums] + [lax.ppermute(sums, "tensor", swap) for swap in Z_SWAPS]
    return rescale(moved, sums, width), new_moment, new_second


def solution(mesh):
    spec = P("dp", "tensor")
    return jax.shard_map(
        on_device,
        mesh=mesh,
        in_specs=(P("dp", None), spec, spec, spec, spec),
        out_specs=(spec, spec, spec),
        check_vma=False,
    )
```

```python
import functools

import jax
import jax.numpy as jnp
from jax import lax
from jax.experimental import pallas as pl
from jax.experimental.pallas import tpu as pltpu
from jax.sharding import PartitionSpec as P

F32 = jnp.float32
BF16 = jnp.bfloat16
MIB = 2**20
VMEM = pltpu.VMEM
ROWS = 64
TILES = 16
STRIPS = 8
FORTH, BACK = (0, 1, 3, 2), (1, 0, 2, 3)
CHAINS = ((0, 0, 768, FORTH), (1, 0, 768, BACK), (0, 768, 256, FORTH), (1, 768, 256, BACK))
PARTS = [sum(chain[2] for chain in CHAINS if chain[0] == part) for part in (0, 1)]
ORDER = (
    "s1:0", "s1:1", "oq:0", "a1:0", "o1:1", "s0:01", "s1:23", "op:0",
    "op:1", "o1:2", "o1:3", "s0:23", "x2:0", "x2:1", "c2:1", "c2:0",
    "o0:2", "o0:3", "c2:3", "c2:2", "c3:13", "c3:02", "c4:1", "c4:0",
    "f:1", "f:0",
)
COSTS = {"x2:1": 20000000000, "c2:0": 10000000000, "f:1": 1000000000}

RING_A = (1, 0, 3, 2)
RING_B = (3, 2, 1, 0)


def device_index(y, x, core):
    return (y * 4 + x) * 2 + core


def swap_pairs(kind):
    partner = RING_B if kind % 2 else RING_A
    pairs = []
    for y in range(4):
        for x in range(4):
            for core in range(2):
                along_x = (core == 0) == (kind < 2)
                to = (y, partner[x]) if along_x else (partner[y], x)
                pairs.append((device_index(y, x, core), device_index(*to, core)))
    return pairs


SWAPS = [swap_pairs(kind) for kind in range(4)]
CORE_SWAP = [(i, i ^ 1) for i in range(32)]
Z_SWAPS = [list(enumerate(ring)) for ring in (RING_A, RING_B, (2, 3, 0, 1))]


def params(mib, **more):
    return pltpu.CompilerParams(vmem_limit_bytes=mib * MIB, **more)


def in_vmem():
    return pl.BlockSpec(memory_space=VMEM)


def gray(i):
    high = i >> 1
    return high ^ (i & 1), high


def half_copies(inputs, half, which, arrived, first):
    rows, width = half.shape[0] // STRIPS, half.shape[1]
    first_col = which * (inputs.shape[1] - width)
    return [
        pltpu.make_async_copy(
            inputs.at[k * rows : (k + 1) * rows, first_col : first_col + width],
            half.at[k * rows : (k + 1) * rows],
            arrived.at[first + k],
        )
        for k in range(STRIPS)
    ]


def prep_kernel(pieces, out_grad, inputs, turned, left, right, product, held, arrived):
    strips = held.shape[0]
    tiles = TILES // strips
    width = tiles * 128
    copies = [
        pltpu.make_async_copy(
            out_grad.at[:, k * width : (k + 1) * width], held.at[k], arrived.at[k]
        )
        for k in range(strips)
    ]
    copies += half_copies(inputs, left, 0, arrived, strips)
    copies += half_copies(inputs, right, 1, arrived, strips + STRIPS)
    for copy in copies:
        copy.start()
    me = lax.axis_index("dp")
    core = me & 1
    my_x = gray((me >> 1) & 3)
    my_y = gray(me >> 3)
    for tile in range(TILES):
        if tile % tiles == 0:
            copies[tile // tiles].wait()
        xa, xb = [a ^ b for a, b in zip(gray(tile & 3), my_x)]
        ya, yb = [a ^ b for a, b in zip(gray(tile >> 2), my_y)]
        place0 = xa * 8 + xb * 4 + ya * 2 + yb + 16 * (1 - core)
        place1 = ya * 8 + yb * 4 + xa * 2 + xb + 16 * core
        col = tile % tiles * 128
        block = held[tile // tiles, :, col : col + 128].T
        turned[pl.ds(place0, 1)] = block[:ROWS][None]
        turned[pl.ds(place1, 1)] = block[ROWS:][None]
    for copy in copies[strips : strips + STRIPS]:
        copy.wait()
    gemm_kernel(pieces, 0, 0, turned, left, right, product)
    for copy in copies[strips + STRIPS :]:
        copy.wait()


def prep(out_grad, inputs, pieces):
    tokens, rows = out_grad.shape
    strips = 8
    parts = [VMEM((tokens, cols), BF16) for cols in PARTS]
    product = sum(hi - lo for (lo, hi), *_ in pieces) * ROWS, pieces[0][3]
    return pl.pallas_call(
        functools.partial(prep_kernel, pieces),
        out_shape=(VMEM((2 * TILES, ROWS, tokens), BF16), *parts, VMEM(product, F32)),
        in_specs=[pl.BlockSpec(memory_space=pl.ANY)] * 2,
        out_specs=[in_vmem()] * 4,
        scratch_shapes=[
            VMEM((strips, tokens, rows // strips), BF16),
            pltpu.SemaphoreType.DMA((strips + 2 * STRIPS,)),
        ],
        compiler_params=params(12),
        name="prep",
    )(out_grad, inputs)


def call(kernel, args, after, flops, **more):
    extra = () if after is None else (after,)

    def run(*refs):
        kernel(*refs[: len(args)], *refs[len(args) + len(extra) :])

    specs = [in_vmem()] * len(args) + [pl.BlockSpec(memory_space=pl.ANY)] * len(extra)
    cost = pl.CostEstimate(flops=flops, bytes_accessed=1, transcendentals=0)
    return pl.pallas_call(run, in_specs=specs, cost_estimate=cost, **more)(*args, *extra)


def gemm_kernel(pieces, offset, count, turned, *refs):
    halves, received, outs = refs[:2], refs[2 : 2 + count], refs[2 + count :]
    row = 0
    for (lo, hi), half, first, width in pieces:
        rows = (hi - lo) * ROWS
        left = turned[lo:hi].reshape(rows, turned.shape[2])
        out, at = outs[row // outs[0].shape[0]], row % outs[0].shape[0]
        for col in range(0, width, 256):
            end = min(col + 256, width)
            right = halves[half][:, first + col : first + end]
            part = jnp.dot(left, right, preferred_element_type=F32)
            if received:
                from_row = offset + row
                ref, come = received[from_row // received[0].shape[0]], from_row % received[0].shape[0]
                part = part + ref[come : come + rows, col:end]
            out[at : at + rows, col:end] = part
        if width < out.shape[1]:
            out[at : at + rows, width:] = jnp.zeros((rows, out.shape[1] - width), F32)
        row += rows


def gemm(name, after, cost, turned, halves, pieces, shares=1, received=(), offset=0):
    rows = sum(hi - lo for (lo, hi), *_ in pieces) * ROWS
    return call(
        functools.partial(gemm_kernel, pieces, offset, len(received)),
        (turned, *halves, *received),
        after,
        cost,
        out_shape=[VMEM((rows // shares, max(piece[3] for piece in pieces)), F32)] * shares,
        out_specs=[in_vmem()] * shares,
        compiler_params=params(4),
        name=name,
    )


def pieces_of(chain, side, sent):
    *columns, order = CHAINS[chain]
    base = 0 if side == "s" else TILES
    if order[0] == 0:
        spans = ((base + 8 * sent, base + 8 * sent + 8),)
    else:
        spans = tuple((lo, lo + 4) for lo in (base + 4 * sent, base + 4 * sent + 8))
    return [(span, *columns) for span in spans]


def quarters(pieces):
    return [((at, at + 4), *columns) for (lo, hi), *columns in pieces for at in range(lo, hi, 4)]


def add_kernel(a, b, out):
    out[...] = a[...] + b[...]


def add(name, after, cost, a, b):
    return call(
        add_kernel,
        (a, b),
        after,
        cost,
        out_shape=VMEM(a.shape, F32),
        out_specs=in_vmem(),
        compiler_params=params(4),
        name=name,
    )


def combine_kernel(split, offset, added, *refs):
    *refs, up, down = refs
    col = 0
    for is_sum in added:
        kept = refs.pop(0)
        came = None if is_sum else refs.pop(0)
        rows, width = kept.shape
        size = rows // (2 * split)
        for i in range(split):
            for half, out in ((0, down), (1, up)):
                lo = (2 * i + half) * size
                total = kept[lo : lo + size]
                if came is not None:
                    total = total + came[offset + lo : offset + lo + size, :width]
                out[i * size : (i + 1) * size, col : col + width] = total
        col += width


def combine(name, after, cost, split, pairs, offset=0):
    half = VMEM((pairs[0][0].shape[0] // 2, sum(kept.shape[1] for kept, _ in pairs)), F32)
    added = [came is None for _, came in pairs]
    return call(
        functools.partial(combine_kernel, split, offset, added),
        [array for pair in pairs for array in pair if array is not None],
        after,
        cost,
        out_shape=(half, half),
        out_specs=[in_vmem()] * 2,
        compiler_params=params(4),
        name=name,
    )


def finish_kernel(first, kept, came, weights, moment, second, *outs):
    moved, new_moment, new_second, sums = outs
    total = jnp.zeros((ROWS, 128), F32)
    for col in range(0, kept.shape[1], 128):
        there = (slice(None), slice(col, col + 128))
        here = (slice(None), slice(first + col, first + col + 128))
        grad = kept[there] + came[there]
        m = 0.9 * moment[here] + 0.1 * grad
        v = 0.95 * second[here] + 0.05 * grad * grad
        step = 0.3 * (m / (1.0 - 0.9**10))
        w = weights[here] - step / (jnp.sqrt(v / (1.0 - 0.95**10)) + 1e-08)
        new_moment[there] = m
        new_second[there] = v
        moved[there] = w
        total = total + w * w
    total = jnp.broadcast_to(jnp.sum(total, axis=1, keepdims=True), total.shape)
    sums[...] = total.T[: sums.shape[0]]


def finish(name, after, cost, first, kept, came, weights, moment, second):
    shape = VMEM(kept.shape, F32)
    return call(
        functools.partial(finish_kernel, first),
        (kept, came, weights, moment, second),
        after,
        cost,
        out_shape=(shape, shape, shape, VMEM((8, ROWS), F32)),
        out_specs=[in_vmem()] * 4,
        compiler_params=params(4),
        name=name,
    )


def join_kernel(a, b, c, d, ab, cd):
    width = a.shape[1]
    for left, right, out in ((a, b, ab), (c, d, cd)):
        out[:, :width] = left[...]
        out[:, width:] = right[...]


def join(after, moments, seconds):
    shape = jax.ShapeDtypeStruct((ROWS, sum(PARTS)), F32)
    return call(
        join_kernel,
        (*moments, *seconds),
        after,
        1,
        out_shape=[shape] * 2,
        out_specs=[in_vmem()] * 2,
        compiler_params=params(4),
        name="join",
    )


def rescale_kernel(width, a, b, *refs):
    *sums, out = refs
    total = sums[0][...]
    for other in sums[1:]:
        total = total + other[...]
    scale = lax.rsqrt(total[:1] / width + 1e-06)
    scale = jnp.broadcast_to(scale, (128, ROWS)).T
    at = 0
    for moved in (a, b):
        for col in range(0, moved.shape[1], 128):
            out[:, at + col : at + col + 128] = moved[:, col : col + 128] * scale
        at += moved.shape[1]


def rescale(moved, sums, width):
    return pl.pallas_call(
        functools.partial(rescale_kernel, width),
        out_shape=jax.ShapeDtypeStruct((ROWS, sum(PARTS)), F32),
        in_specs=[in_vmem()] * (2 + len(sums)),
        out_specs=in_vmem(),
        compiler_params=params(4),
        name="rescale",
    )(*moved, *sums)


def on_device(out_grad, inputs, weights, moment, second):
    width = weights.shape[1] * lax.axis_size("tensor")
    out_grad, inputs = [pltpu.with_memory_space_constraint(z, pltpu.HBM) for z in (out_grad, inputs)]
    first = pieces_of(int(ORDER[0][-1]), "s", 1)
    turned, *halves, product = prep(out_grad, inputs, first)
    n = len(CHAINS)
    received, kept, came = {}, [None] * n, [None] * n
    late, own, done = {}, {}, {}
    last = None
    for item in ORDER:
        what, which = item.split(":")
        which, _, shares = which.partition("/")
        shares = int(shares or 1)
        name = f"{what}_{which}"
        cost = COSTS.get(what + ":" + which, 1)
        chains = [int(i) for i in which]
        i = chains[0]
        order = CHAINS[i][3]
        if what[0] in "so":
            sent = int(what[1] == "1")
            pieces = [piece for j in chains for piece in pieces_of(j, what[0], sent)]
            if what[0] == "s":
                if shares > 1:
                    pieces = quarters(pieces)
                if last is None:
                    parts = [product]
                else:
                    parts = gemm(name, last, cost, turned, halves, pieces, shares)
                last = parts[0]
                over = [lax.ppermute(part, "dp", CORE_SWAP) for part in parts]
                for k, j in enumerate(chains):
                    received[j, sent] = over, k * (TILES // 2) * ROWS
            elif what[1] == "p":
                [last] = gemm(name, last, cost, turned, halves, pieces)
                kept[i] = last
            elif what[1] == "q":
                pieces = pieces_of(i, "o", 1)
                [last] = gemm(name, last, cost, turned, halves, pieces)
                own[i] = last
            else:
                over, offset = received[i, sent]
                if len(over) > 1:
                    pieces = quarters(pieces)
                [last] = gemm(name, last, cost, turned, halves, pieces, 1, over, offset)
                if sent:
                    came[i] = lax.ppermute(last, "dp", SWAPS[order[0]])
                else:
                    kept[i] = last
        elif what == "a1":
            last = add(name, last, cost, own[i], *received[i, 1][0])
            came[i] = lax.ppermute(last, "dp", SWAPS[order[0]])
        elif what[0] == "x":
            last = kept[i] = add(name, last, cost, kept[i], came[i])
            came[i] = None
            if what == "x2":
                [came[i]], late[i] = received[i, 0]
        elif what == "f":
            first = i * PARTS[0]
            done[i] = finish(name, last, cost, first, kept[i], came[i], weights, moment, second)
            last = done[i][3]
        else:
            step = int(what[1])
            split = 2 if step == 3 and order[2] == 3 else 1
            pairs = [(kept[j], came[j]) for j in chains]
            last, kept[i] = combine(name, last, cost, split, pairs, late.pop(i, 0))
            came[i] = lax.ppermute(last, "dp", SWAPS[order[step - 1]])
    moved, moments, seconds, sums = zip(done[0], done[1])
    sums = sums[0] + sums[1]
    new_moment, new_second = join(sums, moments, seconds)
    sums = [sums] + [lax.ppermute(sums, "tensor", swap) for swap in Z_SWAPS]
    return rescale(moved, sums, width), new_moment, new_second


def solution(mesh):
    spec = P("dp", "tensor")
    return jax.shard_map(
        on_device,
        mesh=mesh,
        in_specs=(P("dp", None), spec, spec, spec, spec),
        out_specs=(spec, spec, spec),
        check_vma=False,
    )
```

```python
import functools

import jax
import jax.numpy as jnp
from jax import lax
from jax.experimental import pallas as pl
from jax.experimental.pallas import tpu as pltpu
from jax.sharding import PartitionSpec as P

F32 = jnp.float32
BF16 = jnp.bfloat16
MIB = 2**20
VMEM = pltpu.VMEM
ROWS = 64
TILES = 16
STRIPS = 8
FORTH, BACK = (0, 1, 3, 2), (1, 0, 2, 3)
CHAINS = ((0, 0, 768, FORTH), (1, 0, 768, BACK), (0, 768, 256, FORTH), (1, 768, 256, BACK))
PARTS = [sum(chain[2] for chain in CHAINS if chain[0] == part) for part in (0, 1)]
ORDER = (
    "s1:0", "s1:1", "oq:0", "a1:0", "o1:1", "s0:01", "s1:23", "op:0",
    "op:1", "o1:2", "o1:3", "s0:23", "x2:0", "x2:1", "c2:1", "c2:0",
    "o0:2", "o0:3", "c2:3", "c2:2", "c3:13", "c3:02", "c4:1", "c4:0",
    "f:1", "f:0",
)
COSTS = {"x2:1": 20000000000, "c2:0": 10000000000, "f:1": 1000000000}

RING_A = (1, 0, 3, 2)
RING_B = (3, 2, 1, 0)


def device_index(y, x, core):
    return (y * 4 + x) * 2 + core


def swap_pairs(kind):
    partner = RING_B if kind % 2 else RING_A
    pairs = []
    for y in range(4):
        for x in range(4):
            for core in range(2):
                along_x = (core == 0) == (kind < 2)
                to = (y, partner[x]) if along_x else (partner[y], x)
                pairs.append((device_index(y, x, core), device_index(*to, core)))
    return pairs


SWAPS = [swap_pairs(kind) for kind in range(4)]
CORE_SWAP = [(i, i ^ 1) for i in range(32)]
Z_SWAPS = [list(enumerate(ring)) for ring in (RING_A, RING_B, (2, 3, 0, 1))]


def params(mib, **more):
    return pltpu.CompilerParams(vmem_limit_bytes=mib * MIB, **more)


def in_vmem():
    return pl.BlockSpec(memory_space=VMEM)


def gray(i):
    high = i >> 1
    return high ^ (i & 1), high


def half_copies(inputs, half, which, arrived, first, lo, hi):
    rows = half.shape[0] // STRIPS
    first_col = which * (inputs.shape[1] - half.shape[1])
    return [
        pltpu.make_async_copy(
            inputs.at[k * rows : (k + 1) * rows, first_col + lo : first_col + hi],
            half.at[k * rows : (k + 1) * rows, lo:hi],
            arrived.at[first + k],
        )
        for k in range(STRIPS)
    ]


def prep_kernel(pieces, out_grad, inputs, turned, left, right, product, held, arrived):
    strips = held.shape[0]
    tiles = TILES // strips
    width = tiles * 128
    copies = [
        pltpu.make_async_copy(
            out_grad.at[:, k * width : (k + 1) * width], held.at[k], arrived.at[k]
        )
        for k in range(strips)
    ]
    cut = pieces[0][3]
    copies += half_copies(inputs, left, 0, arrived, strips, 0, cut)
    copies += half_copies(inputs, right, 1, arrived, strips + STRIPS, 0, right.shape[1])
    copies += half_copies(inputs, left, 0, arrived, strips + 2 * STRIPS, cut, left.shape[1])
    for copy in copies:
        copy.start()
    me = lax.axis_index("dp")
    core = me & 1
    my_x = gray((me >> 1) & 3)
    my_y = gray(me >> 3)
    for tile in range(TILES):
        if tile % tiles == 0:
            copies[tile // tiles].wait()
        xa, xb = [a ^ b for a, b in zip(gray(tile & 3), my_x)]
        ya, yb = [a ^ b for a, b in zip(gray(tile >> 2), my_y)]
        place0 = xa * 8 + xb * 4 + ya * 2 + yb + 16 * (1 - core)
        place1 = ya * 8 + yb * 4 + xa * 2 + xb + 16 * core
        col = tile % tiles * 128
        block = held[tile // tiles, :, col : col + 128].T
        turned[pl.ds(place0, 1)] = block[:ROWS][None]
        turned[pl.ds(place1, 1)] = block[ROWS:][None]
    for copy in copies[strips : strips + STRIPS]:
        copy.wait()
    gemm_kernel(pieces, 0, 0, turned, left, right, product)
    for copy in copies[strips + STRIPS :]:
        copy.wait()


def prep(out_grad, inputs, pieces):
    tokens, rows = out_grad.shape
    strips = 8
    parts = [VMEM((tokens, cols), BF16) for cols in PARTS]
    product = sum(hi - lo for (lo, hi), *_ in pieces) * ROWS, pieces[0][3]
    return pl.pallas_call(
        functools.partial(prep_kernel, pieces),
        out_shape=(VMEM((2 * TILES, ROWS, tokens), BF16), *parts, VMEM(product, F32)),
        in_specs=[pl.BlockSpec(memory_space=pl.ANY)] * 2,
        out_specs=[in_vmem()] * 4,
        scratch_shapes=[
            VMEM((strips, tokens, rows // strips), BF16),
            pltpu.SemaphoreType.DMA((strips + 3 * STRIPS,)),
        ],
        compiler_params=params(12),
        name="prep",
    )(out_grad, inputs)


def call(kernel, args, after, flops, **more):
    extra = () if after is None else (after,)

    def run(*refs):
        kernel(*refs[: len(args)], *refs[len(args) + len(extra) :])

    specs = [in_vmem()] * len(args) + [pl.BlockSpec(memory_space=pl.ANY)] * len(extra)
    cost = pl.CostEstimate(flops=flops, bytes_accessed=1, transcendentals=0)
    return pl.pallas_call(run, in_specs=specs, cost_estimate=cost, **more)(*args, *extra)


def gemm_kernel(pieces, offset, count, turned, *refs):
    halves, received, outs = refs[:2], refs[2 : 2 + count], refs[2 + count :]
    row = 0
    for (lo, hi), half, first, width in pieces:
        rows = (hi - lo) * ROWS
        left = turned[lo:hi].reshape(rows, turned.shape[2])
        out, at = outs[row // outs[0].shape[0]], row % outs[0].shape[0]
        for col in range(0, width, 256):
            end = min(col + 256, width)
            right = halves[half][:, first + col : first + end]
            part = jnp.dot(left, right, preferred_element_type=F32)
            if received:
                from_row = offset + row
                ref, come = received[from_row // received[0].shape[0]], from_row % received[0].shape[0]
                part = part + ref[come : come + rows, col:end]
            out[at : at + rows, col:end] = part
        if width < out.shape[1]:
            out[at : at + rows, width:] = jnp.zeros((rows, out.shape[1] - width), F32)
        row += rows


def gemm(name, after, cost, turned, halves, pieces, shares=1, received=(), offset=0):
    rows = sum(hi - lo for (lo, hi), *_ in pieces) * ROWS
    return call(
        functools.partial(gemm_kernel, pieces, offset, len(received)),
        (turned, *halves, *received),
        after,
        cost,
        out_shape=[VMEM((rows // shares, max(piece[3] for piece in pieces)), F32)] * shares,
        out_specs=[in_vmem()] * shares,
        compiler_params=params(4),
        name=name,
    )


def pieces_of(chain, side, sent):
    *columns, order = CHAINS[chain]
    base = 0 if side == "s" else TILES
    if order[0] == 0:
        spans = ((base + 8 * sent, base + 8 * sent + 8),)
    else:
        spans = tuple((lo, lo + 4) for lo in (base + 4 * sent, base + 4 * sent + 8))
    return [(span, *columns) for span in spans]


def quarters(pieces):
    return [((at, at + 4), *columns) for (lo, hi), *columns in pieces for at in range(lo, hi, 4)]


def add_kernel(a, b, out):
    out[...] = a[...] + b[...]


def add(name, after, cost, a, b):
    return call(
        add_kernel,
        (a, b),
        after,
        cost,
        out_shape=VMEM(a.shape, F32),
        out_specs=in_vmem(),
        compiler_params=params(4),
        name=name,
    )


def combine_kernel(split, offset, added, *refs):
    *refs, up, down = refs
    col = 0
    for is_sum in added:
        kept = refs.pop(0)
        came = None if is_sum else refs.pop(0)
        rows, width = kept.shape
        size = rows // (2 * split)
        for i in range(split):
            for half, out in ((0, down), (1, up)):
                lo = (2 * i + half) * size
                total = kept[lo : lo + size]
                if came is not None:
                    total = total + came[offset + lo : offset + lo + size, :width]
                out[i * size : (i + 1) * size, col : col + width] = total
        col += width


def combine(name, after, cost, split, pairs, offset=0):
    half = VMEM((pairs[0][0].shape[0] // 2, sum(kept.shape[1] for kept, _ in pairs)), F32)
    added = [came is None for _, came in pairs]
    return call(
        functools.partial(combine_kernel, split, offset, added),
        [array for pair in pairs for array in pair if array is not None],
        after,
        cost,
        out_shape=(half, half),
        out_specs=[in_vmem()] * 2,
        compiler_params=params(4),
        name=name,
    )


def finish_kernel(first, kept, came, weights, moment, second, *outs):
    moved, new_moment, new_second, sums = outs
    total = jnp.zeros((ROWS, 128), F32)
    for col in range(0, kept.shape[1], 128):
        there = (slice(None), slice(col, col + 128))
        here = (slice(None), slice(first + col, first + col + 128))
        grad = kept[there] + came[there]
        m = 0.9 * moment[here] + 0.1 * grad
        v = 0.95 * second[here] + 0.05 * grad * grad
        step = 0.3 * (m / (1.0 - 0.9**10))
        w = weights[here] - step / (jnp.sqrt(v / (1.0 - 0.95**10)) + 1e-08)
        new_moment[there] = m
        new_second[there] = v
        moved[there] = w
        total = total + w * w
    total = jnp.broadcast_to(jnp.sum(total, axis=1, keepdims=True), total.shape)
    sums[...] = total.T[: sums.shape[0]]


def finish(name, after, cost, first, kept, came, weights, moment, second):
    shape = VMEM(kept.shape, F32)
    return call(
        functools.partial(finish_kernel, first),
        (kept, came, weights, moment, second),
        after,
        cost,
        out_shape=(shape, shape, shape, VMEM((8, ROWS), F32)),
        out_specs=[in_vmem()] * 4,
        compiler_params=params(4),
        name=name,
    )


def join_kernel(a, b, c, d, ab, cd):
    width = a.shape[1]
    for left, right, out in ((a, b, ab), (c, d, cd)):
        out[:, :width] = left[...]
        out[:, width:] = right[...]


def join(after, moments, seconds):
    shape = jax.ShapeDtypeStruct((ROWS, sum(PARTS)), F32)
    return call(
        join_kernel,
        (*moments, *seconds),
        after,
        1,
        out_shape=[shape] * 2,
        out_specs=[in_vmem()] * 2,
        compiler_params=params(4),
        name="join",
    )


def rescale_kernel(width, a, b, *refs):
    *sums, out = refs
    total = sums[0][...]
    for other in sums[1:]:
        total = total + other[...]
    scale = lax.rsqrt(total[:1] / width + 1e-06)
    scale = jnp.broadcast_to(scale, (128, ROWS)).T
    at = 0
    for moved in (a, b):
        for col in range(0, moved.shape[1], 128):
            out[:, at + col : at + col + 128] = moved[:, col : col + 128] * scale
        at += moved.shape[1]


def rescale(moved, sums, width):
    return pl.pallas_call(
        functools.partial(rescale_kernel, width),
        out_shape=jax.ShapeDtypeStruct((ROWS, sum(PARTS)), F32),
        in_specs=[in_vmem()] * (2 + len(sums)),
        out_specs=in_vmem(),
        compiler_params=params(4),
        name="rescale",
    )(*moved, *sums)


def on_device(out_grad, inputs, weights, moment, second):
    width = weights.shape[1] * lax.axis_size("tensor")
    out_grad, inputs = [pltpu.with_memory_space_constraint(z, pltpu.HBM) for z in (out_grad, inputs)]
    first = pieces_of(int(ORDER[0][-1]), "s", 1)
    turned, *halves, product = prep(out_grad, inputs, first)
    n = len(CHAINS)
    received, kept, came = {}, [None] * n, [None] * n
    late, own, done = {}, {}, {}
    last = None
    for item in ORDER:
        what, which = item.split(":")
        which, _, shares = which.partition("/")
        shares = int(shares or 1)
        name = f"{what}_{which}"
        cost = COSTS.get(what + ":" + which, 1)
        chains = [int(i) for i in which]
        i = chains[0]
        order = CHAINS[i][3]
        if what[0] in "so":
            sent = int(what[1] == "1")
            pieces = [piece for j in chains for piece in pieces_of(j, what[0], sent)]
            if what[0] == "s":
                if shares > 1:
                    pieces = quarters(pieces)
                if last is None:
                    parts = [product]
                else:
                    parts = gemm(name, last, cost, turned, halves, pieces, shares)
                last = parts[0]
                over = [lax.ppermute(part, "dp", CORE_SWAP) for part in parts]
                for k, j in enumerate(chains):
                    received[j, sent] = over, k * (TILES // 2) * ROWS
            elif what[1] == "p":
                [last] = gemm(name, last, cost, turned, halves, pieces)
                kept[i] = last
            elif what[1] == "q":
                pieces = pieces_of(i, "o", 1)
                [last] = gemm(name, last, cost, turned, halves, pieces)
                own[i] = last
            else:
                over, offset = received[i, sent]
                if len(over) > 1:
                    pieces = quarters(pieces)
                [last] = gemm(name, last, cost, turned, halves, pieces, 1, over, offset)
                if sent:
                    came[i] = lax.ppermute(last, "dp", SWAPS[order[0]])
                else:
                    kept[i] = last
        elif what == "a1":
            last = add(name, last, cost, own[i], *received[i, 1][0])
            came[i] = lax.ppermute(last, "dp", SWAPS[order[0]])
        elif what[0] == "x":
            last = kept[i] = add(name, last, cost, kept[i], came[i])
            came[i] = None
            if what == "x2":
                [came[i]], late[i] = received[i, 0]
        elif what == "f":
            first = i * PARTS[0]
            done[i] = finish(name, last, cost, first, kept[i], came[i], weights, moment, second)
            last = done[i][3]
        else:
            step = int(what[1])
            split = 2 if step == 3 and order[2] == 3 else 1
            pairs = [(kept[j], came[j]) for j in chains]
            last, kept[i] = combine(name, last, cost, split, pairs, late.pop(i, 0))
            came[i] = lax.ppermute(last, "dp", SWAPS[order[step - 1]])
    moved, moments, seconds, sums = zip(done[0], done[1])
    sums = sums[0] + sums[1]
    new_moment, new_second = join(sums, moments, seconds)
    sums = [sums] + [lax.ppermute(sums, "tensor", swap) for swap in Z_SWAPS]
    return rescale(moved, sums, width), new_moment, new_second


def solution(mesh):
    spec = P("dp", "tensor")
    return jax.shard_map(
        on_device,
        mesh=mesh,
        in_specs=(P("dp", None), spec, spec, spec, spec),
        out_specs=(spec, spec, spec),
        check_vma=False,
    )
```
